768 devices in a mesh: dp: 48 (over y, z_lo, core), fsdp: 16 (over z_hi, x).
Axes of the slice: x: 4, y: 8, z: 12 (z_hi: 4, z_lo: 3; z = z_hi * 3 + z_lo), core: 2. Of those that a mesh axis runs over, the one named last changes fastest.
Arguments:
- tokens: bfloat16 [768, 8192], P(None, 'fsdp'), may hold values from -6 to 6
- targets: bfloat16 [768, 8192], P(None, 'fsdp'), may hold values from -6 to 6
- gate_weights: bfloat16 [2, 12288, 8192], P(None, 'dp', 'fsdp'), may hold values from -6 to 6
- up_weights: bfloat16 [2, 12288, 8192], P(None, 'dp', 'fsdp'), may hold values from -6 to 6
- means: float32 [12288, 8192], P('dp', 'fsdp'), may hold values from -6 to 6
- hessian: float32 [12288, 8192], P('dp', 'fsdp'), may hold values from 0.1 to 1
- momentum: float32 [12288, 8192], P('dp', 'fsdp'), may hold values from -4 to 4
- noise: bfloat16 [2, 12288, 8192], P(None, 'dp', 'fsdp'), may hold values from -6 to 6
Outputs:
- new_means: float32 [12288, 8192], P('dp', 'fsdp')
- new_hessian: float32 [12288, 8192], P('dp', 'fsdp')
- new_momentum: float32 [12288, 8192], P('dp', 'fsdp')
The draws below stay inside these ranges and needn't reach their ends.
All inputs are finite; a program needn't handle non-finite values.
Results may differ from the reference program's by a relative error of at most 0.013.
Values may be sent and summed in bfloat16 or wider, within the bound.
No kernel may reach another device: no remote copies, remote signals or barrier semaphores. Data moves between devices by JAX's collectives and lax.ppermute only.
A program may use at most 32 MiB of HBM per device.

```python
import math
import jax
import jax.numpy as jnp

D = 8192
H = 12288
TOKENS = 768


def level_of(key, dims, pieces, smallest, largest):
    loudness = 1.0
    for position, parts in pieces:
        draws = jax.random.uniform(jax.random.fold_in(jax.random.fold_in(key, 6), position), (parts,), jnp.float32, smallest / len(pieces), largest / len(pieces))
        loudness = loudness * jnp.repeat(jnp.exp(draws), dims[position] // parts).reshape((-1,) + (1,) * (len(dims) - 1 - position))
    return loudness


def centred(stream_key, dims, width, limit, split=(), held_as=jnp.bfloat16):
    level = level_of(stream_key, dims, split, -0.22, 0.18) if split else 1.0
    result = jax.random.normal(stream_key, dims, jnp.float32) * width * level
    return jnp.minimum(jnp.maximum(result, -limit), limit).astype(held_as)


def setup_inputs(seed: int = 0) -> dict:
    key_list = jax.random.split(jax.random.key(seed), 9)
    tokens = centred(key_list[0], (TOKENS, D), 1.0, 6.0, ((1, 16),))
    targets = centred(key_list[1], (TOKENS, D), 1.0, 6.0, ((1, 16),))
    gate_weights = centred(key_list[2], (2, H, D), 1.0, 6.0, ((1, 48), (2, 16)))
    up_weights = centred(key_list[3], (2, H, D), 1.0, 6.0, ((1, 48), (2, 16)))
    means = centred(key_list[4], (H, D), 1.0, 6.0, ((0, 48), (1, 16)), jnp.float32)
    hessian = jnp.clip(jnp.exp(math.log(1.0) - 2.3025851 * jax.random.uniform(key_list[5], (H, D), jnp.float32) ** level_of(key_list[5], (H, D), ((0, 48), (1, 16)), -0.2, 0.2)), 0.1, 1.0)
    momentum = centred(key_list[6], (H, D), 0.3, 4.0, ((0, 48), (1, 16)), jnp.float32)
    noise = centred(key_list[7], (2, H, D), 1.0, 6.0, ((1, 48), (2, 16)))
    return dict(tokens=tokens, targets=targets, gate_weights=gate_weights, up_weights=up_weights, means=means, hessian=hessian, momentum=momentum, noise=noise)


prior_size = 16.0
weight_decay = 0.001
beta_one = 0.9
beta_two = 0.95
step_rate = 0.2
loss_gain = 300.0

def sample_grad(tokens, targets, gate_weight, up_weight, down_weight):
    scale_in = 1.0 / math.sqrt(D)
    scale_out = 1.0 / math.sqrt(H)
    gate_sum = jnp.dot(tokens, gate_weight.T, preferred_element_type=jnp.float32) * scale_in
    up_sum = jnp.dot(tokens, up_weight.T, preferred_element_type=jnp.float32) * scale_in
    sigmoid_gate = jax.nn.sigmoid(gate_sum)
    hidden = (gate_sum * sigmoid_gate * up_sum).astype(jnp.bfloat16)
    output = jnp.dot(hidden, down_weight, preferred_element_type=jnp.float32) * scale_out
    d_out = (loss_gain / math.sqrt(TOKENS) * (output - targets.astype(jnp.float32))).astype(jnp.bfloat16)
    return jnp.dot(hidden.T, d_out, preferred_element_type=jnp.float32) * scale_out

def reference(tokens, targets, gate_weights, up_weights, means, hessian, momentum, noise):
    inv_sigma = jnp.sqrt(prior_size * (hessian + weight_decay))
    noise_f = noise.astype(jnp.float32)
    first_grad = sample_grad(tokens, targets, gate_weights[0], up_weights[0], (means + noise_f[0] / inv_sigma).astype(jnp.bfloat16))
    second_grad = sample_grad(tokens, targets, gate_weights[1], up_weights[1], (means + noise_f[1] / inv_sigma).astype(jnp.bfloat16))
    grad_mean = 0.5 * (first_grad + second_grad)
    curv_mean = 0.5 * (first_grad * noise_f[0] + second_grad * noise_f[1]) * inv_sigma
    new_momentum = beta_one * momentum + (1.0 - beta_one) * grad_mean
    spread = hessian - curv_mean
    new_hessian = beta_two * hessian + (1.0 - beta_two) * curv_mean + 0.5 * (1.0 - beta_two) ** 2 * spread * spread / (hessian + weight_decay)
    new_means = means - step_rate * (new_momentum + weight_decay * means) / (new_hessian + weight_decay)
    return (new_means, new_hessian, new_momentum)
```

```python
import math

import jax
import jax.numpy as jnp
from jax import lax
from jax.sharding import Mesh, PartitionSpec as P

D = 8192


prior_size = 16.0
weight_decay = 0.001
beta_one = 0.9
beta_two = 0.95
step_rate = 0.2
loss_gain = 300.0

bf16 = jnp.bfloat16
f32 = jnp.float32
SWAP = [(0, 1), (1, 0)]


def exchange_sum(parts, axis):
    return jnp.sum(lax.all_to_all(parts, axis, 0, 0, tiled=True).astype(f32), axis=0)


def shards(tokens, targets, gate_weights, up_weights, means, hessian, momentum, noise):
    token_count = tokens.shape[0]
    width = tokens.shape[1]
    unit_count = means.shape[0]
    size_x, size_zh = lax.axis_size("x"), lax.axis_size("zh")
    size_y, size_zl, size_c = lax.axis_size("y"), lax.axis_size("zl"), lax.axis_size("c")
    hidden_count = unit_count * size_y * size_zl * size_c
    scale_in = 1.0 / math.sqrt(D)
    scale_out = 1.0 / math.sqrt(hidden_count)
    error_gain = loss_gain / math.sqrt(token_count)
    both = 2 * unit_count

    inv_sigma = jnp.sqrt(prior_size * (hessian + weight_decay))
    noise_f = noise.astype(f32)
    samples = (means[None] + noise_f / inv_sigma[None]).astype(bf16)

    gate_term = jnp.dot(tokens, gate_weights.reshape(both, width).T, preferred_element_type=f32)
    up_term = jnp.dot(tokens, up_weights.reshape(both, width).T, preferred_element_type=f32)
    terms = jnp.concatenate([gate_term.astype(bf16), up_term.astype(bf16)], axis=1)
    terms = exchange_sum(terms.reshape(size_x, -1, 2 * both), "x").astype(bf16)
    sums = exchange_sum(terms.reshape(size_zh, -1, 2 * both), "zh") * scale_in
    gate_sum, up_sum = sums[:, :both], sums[:, both:]
    hidden_share = (gate_sum * jax.nn.sigmoid(gate_sum) * up_sum).astype(bf16)
    hidden = lax.all_gather(hidden_share, "zh", axis=0, tiled=True)
    hidden = lax.all_gather(hidden, "x", axis=0, tiled=True)

    half = token_count // size_c
    core = lax.axis_index("c")
    hidden_own = lax.dynamic_slice_in_dim(hidden, core * half, half, 0)
    hidden_other = lax.dynamic_slice_in_dim(hidden, (1 - core) * half, half, 0)

    def project(rows):
        return jnp.concatenate(
            [
                jnp.dot(rows[:, s * unit_count : (s + 1) * unit_count], samples[s], preferred_element_type=f32)
                for s in range(2)
            ],
            axis=1,
        )

    arrived = lax.ppermute(project(hidden_other).astype(bf16), "c", SWAP)
    out_half = (project(hidden_own) + arrived.astype(f32)).astype(bf16)
    rows_share = half // (size_y * size_zl)
    out_share = exchange_sum(out_half.reshape(size_y * size_zl, rows_share, 2 * width), ("y", "zl")) * scale_out
    first_row = core * half + (lax.axis_index("y") * size_zl + lax.axis_index("zl")) * rows_share
    goal = lax.dynamic_slice_in_dim(targets, first_row, rows_share, 0).astype(f32)
    goal = jnp.concatenate([goal, goal], axis=1)
    d_share = (error_gain * (out_share - goal)).astype(bf16)
    d_own = lax.all_gather(d_share, ("y", "zl"), axis=0, tiled=True)
    d_other = lax.ppermute(d_own, "c", SWAP)

    sample_grads = []
    for s in range(2):
        units = slice(s * unit_count, (s + 1) * unit_count)
        places = slice(s * width, (s + 1) * width)
        own = jnp.dot(hidden_own[:, units].T, d_own[:, places], preferred_element_type=f32)
        other = jnp.dot(hidden_other[:, units].T, d_other[:, places], preferred_element_type=f32)
        sample_grads.append((own + other) * scale_out)
    grad_mean = 0.5 * (sample_grads[0] + sample_grads[1])
    curv_mean = 0.5 * (sample_grads[0] * noise_f[0] + sample_grads[1] * noise_f[1]) * inv_sigma
    new_momentum = beta_one * momentum + (1.0 - beta_one) * grad_mean
    spread = hessian - curv_mean
    new_hessian = (
        beta_two * hessian
        + (1.0 - beta_two) * curv_mean
        + 0.5 * (1.0 - beta_two) ** 2 * spread * spread / (hessian + weight_decay)
    )
    new_means = means - step_rate * (new_momentum + weight_decay * means) / (
        new_hessian + weight_decay
    )
    return (new_means, new_hessian, new_momentum)


def solution(mesh):
    fine = Mesh(mesh.devices.reshape(8, 3, 2, 4, 4), ("y", "zl", "c", "zh", "x"))
    dp, fsdp = ("y", "zl", "c"), ("zh", "x")
    in_specs = (
        P(None, fsdp),
        P(None, fsdp),
        P(None, dp, fsdp),
        P(None, dp, fsdp),
        P(dp, fsdp),
        P(dp, fsdp),
        P(dp, fsdp),
        P(None, dp, fsdp),
    )
    out_specs = (P(dp, fsdp), P(dp, fsdp), P(dp, fsdp))
    return jax.shard_map(shards, mesh=fine, in_specs=in_specs, out_specs=out_specs, check_vma=False)
```

```python
import math

import jax
import jax.numpy as jnp
from jax import lax
from jax.experimental import pallas as pl
from jax.experimental.pallas import tpu as pltpu
from jax.sharding import Mesh, PartitionSpec as P

D = 8192


prior_size = 16.0
weight_decay = 0.001
beta_one = 0.9
beta_two = 0.95
step_rate = 0.2
loss_gain = 300.0

bf16 = jnp.bfloat16
f32 = jnp.float32
SWAP = [(0, 1), (1, 0)]
ROWS = 16


def trade(parts, axis):
    return lax.all_to_all(parts, axis, 0, 0, tiled=True)


def terms_kernel(tokens_ref, gate_ref, up_ref, terms_ref):
    rows = tokens_ref[...]
    both = gate_ref.shape[0]
    for place, weights_ref in ((0, gate_ref), (both, up_ref)):
        terms_ref[:, place : place + both] = lax.dot_general(
            rows, weights_ref[...], (((1,), (1,)), ((), ())), preferred_element_type=f32
        ).astype(bf16)


def gate_up_terms(tokens, gate_weights, up_weights, blocks):
    count, width = tokens.shape
    both = gate_weights.shape[0]
    return pl.pallas_call(
        terms_kernel,
        grid=(blocks,),
        in_specs=[
            pl.BlockSpec((count // blocks, width), lambda i: (i, 0)),
            pl.BlockSpec((both, width), lambda i: (0, 0)),
            pl.BlockSpec((both, width), lambda i: (0, 0)),
        ],
        out_specs=pl.BlockSpec((count // blocks, 2 * both), lambda i: (i, 0)),
        out_shape=jax.ShapeDtypeStruct((count, 2 * both), bf16),
        compiler_params=pltpu.CompilerParams(vmem_limit_bytes=16 * 1024 * 1024),
    )(tokens, gate_weights, up_weights)


def shards(tokens, targets, gate_weights, up_weights, means, hessian, momentum, noise):
    token_count = tokens.shape[0]
    width = tokens.shape[1]
    unit_count = means.shape[0]
    size_x, size_zh = lax.axis_size("x"), lax.axis_size("zh")
    size_y, size_zl, size_c = lax.axis_size("y"), lax.axis_size("zl"), lax.axis_size("c")
    hidden_count = unit_count * size_y * size_zl * size_c
    scale_in = 1.0 / math.sqrt(D)
    scale_out = 1.0 / math.sqrt(hidden_count)
    error_gain = loss_gain / math.sqrt(token_count)
    both = 2 * unit_count
    core = lax.axis_index("c")

    inv_sigma = jnp.sqrt(prior_size * (hessian + weight_decay))
    noise_f = noise.astype(f32)
    samples = (means[None] + noise_f / inv_sigma[None]).astype(bf16)
    weights_own = lax.dynamic_index_in_dim(samples, core, 0, False)
    weights_other = lax.ppermute(lax.dynamic_index_in_dim(samples, 1 - core, 0, False), "c", SWAP)

    terms = gate_up_terms(
        tokens, gate_weights.reshape(both, width), up_weights.reshape(both, width), size_x
    )
    terms = trade(terms.reshape(size_x, -1, 2 * both), "x")
    terms = jnp.sum(terms.astype(f32), axis=0).astype(bf16)
    terms = trade(terms.reshape(size_zh, -1, 2 * both), "zh")
    sums = jnp.sum(terms.astype(f32), axis=0) * scale_in
    gate_sum, up_sum = sums[:, :both], sums[:, both:]
    hidden_share = (gate_sum * jax.nn.sigmoid(gate_sum) * up_sum).astype(bf16)
    share = hidden_share.shape[0]
    out_parts = jnp.stack([hidden_share[:, :unit_count], hidden_share[:, unit_count:]])
    out_parts = jnp.broadcast_to(out_parts[:, None], (size_c, size_zh * size_x, share, unit_count))
    hidden = trade(out_parts.reshape(-1, share, unit_count), ("c", "zh", "x"))
    hidden = hidden.reshape(size_c, token_count, unit_count)
    hidden_own = lax.dynamic_index_in_dim(hidden, core, 0, False)
    hidden_other = lax.dynamic_index_in_dim(hidden, 1 - core, 0, False)

    partial = jnp.dot(hidden_own, weights_own, preferred_element_type=f32) + jnp.dot(
        hidden_other, weights_other, preferred_element_type=f32
    )
    chips = size_y * size_zl
    rows_share = token_count // chips
    partial = trade(partial.astype(bf16).reshape(chips, rows_share, width), ("y", "zl"))
    out_share = jnp.sum(partial.astype(f32), axis=0) * scale_out
    chip = lax.axis_index("y") * size_zl + lax.axis_index("zl")
    per_share = share // ROWS
    goal = []
    for piece in range(rows_share // ROWS):
        place = chip * (rows_share // ROWS) + piece
        owner = place // per_share
        first_row = (
            (owner % size_x) * (token_count // size_x)
            + (owner // size_x) * share
            + (place % per_share) * ROWS
        )
        goal.append(lax.dynamic_slice_in_dim(targets, first_row, ROWS, 0))
    goal = jnp.concatenate(goal, axis=0).astype(f32)
    d_share = (error_gain * (out_share - goal)).astype(bf16)
    d_out = trade(jnp.broadcast_to(d_share[None], (chips, rows_share, width)), ("y", "zl"))
    d_out = d_out.reshape(token_count, width)

    def grad(hidden_part):
        return jnp.dot(hidden_part.T, d_out, preferred_element_type=f32) * scale_out

    grad_other = lax.ppermute(grad(hidden_other), "c", SWAP)
    grad_own = grad(hidden_own)
    noise_own = lax.dynamic_index_in_dim(noise, core, 0, False).astype(f32)
    noise_other = lax.dynamic_index_in_dim(noise, 1 - core, 0, False).astype(f32)
    grad_mean = 0.5 * (grad_own + grad_other)
    curv_mean = 0.5 * (grad_own * noise_own + grad_other * noise_other) * inv_sigma
    new_momentum = beta_one * momentum + (1.0 - beta_one) * grad_mean
    spread = hessian - curv_mean
    new_hessian = (
        beta_two * hessian
        + (1.0 - beta_two) * curv_mean
        + 0.5 * (1.0 - beta_two) ** 2 * spread * spread / (hessian + weight_decay)
    )
    new_means = means - step_rate * (new_momentum + weight_decay * means) / (
        new_hessian + weight_decay
    )
    return (new_means, new_hessian, new_momentum)


def solution(mesh):
    fine = Mesh(mesh.devices.reshape(8, 3, 2, 4, 4), ("y", "zl", "c", "zh", "x"))
    dp, fsdp = ("y", "zl", "c"), ("zh", "x")
    in_specs = (
        P(None, fsdp),
        P(None, fsdp),
        P(None, dp, fsdp),
        P(None, dp, fsdp),
        P(dp, fsdp),
        P(dp, fsdp),
        P(dp, fsdp),
        P(None, dp, fsdp),
    )
    out_specs = (P(dp, fsdp), P(dp, fsdp), P(dp, fsdp))
    return jax.shard_map(shards, mesh=fine, in_specs=in_specs, out_specs=out_specs, check_vma=False)
```

```python
import math

import jax
import jax.numpy as jnp
from jax import lax
from jax.experimental import pallas as pl
from jax.experimental.pallas import tpu as pltpu
from jax.sharding import Mesh, PartitionSpec as P

D = 8192


prior_size = 16.0
weight_decay = 0.001
beta_one = 0.9
beta_two = 0.95
step_rate = 0.2
loss_gain = 300.0

bf16 = jnp.bfloat16
f32 = jnp.float32
SWAP = [(0, 1), (1, 0)]


def trade(parts, axis):
    return lax.all_to_all(parts, axis, 0, 0, tiled=True)


def terms_kernel(tokens_ref, gate_ref, up_ref, terms_ref):
    rows = tokens_ref[...]
    both = gate_ref.shape[0]
    for place, weights_ref in ((0, gate_ref), (both, up_ref)):
        terms_ref[:, place : place + both] = lax.dot_general(
            rows, weights_ref[...], (((1,), (1,)), ((), ())), preferred_element_type=f32
        ).astype(bf16)


def gate_up_terms(tokens, gate_weights, up_weights, blocks):
    count, width = tokens.shape
    both = gate_weights.shape[0]
    return pl.pallas_call(
        terms_kernel,
        grid=(blocks,),
        in_specs=[
            pl.BlockSpec((count // blocks, width), lambda i: (i, 0)),
            pl.BlockSpec((both, width), lambda i: (0, 0)),
            pl.BlockSpec((both, width), lambda i: (0, 0)),
        ],
        out_specs=pl.BlockSpec((count // blocks, 2 * both), lambda i: (i, 0)),
        out_shape=jax.ShapeDtypeStruct((count, 2 * both), bf16),
        compiler_params=pltpu.CompilerParams(vmem_limit_bytes=56 * 1024 * 1024),
    )(tokens, gate_weights, up_weights)


def shards(tokens, targets, gate_weights, up_weights, means, hessian, momentum, noise):
    token_count = tokens.shape[0]
    width = tokens.shape[1]
    unit_count = means.shape[0]
    size_x, size_zh = lax.axis_size("x"), lax.axis_size("zh")
    size_y, size_zl, size_c = lax.axis_size("y"), lax.axis_size("zl"), lax.axis_size("c")
    hidden_count = unit_count * size_y * size_zl * size_c
    scale_in = 1.0 / math.sqrt(D)
    scale_out = 1.0 / math.sqrt(hidden_count)
    error_gain = loss_gain / math.sqrt(token_count)
    both = 2 * unit_count
    core = lax.axis_index("c")

    inv_sigma = jnp.sqrt(prior_size * (hessian + weight_decay))
    noise_f = noise.astype(f32)
    samples = (means[None] + noise_f / inv_sigma[None]).astype(bf16)
    weights_own = lax.dynamic_index_in_dim(samples, core, 0, False)
    weights_other = lax.ppermute(lax.dynamic_index_in_dim(samples, 1 - core, 0, False), "c", SWAP)

    terms = gate_up_terms(
        tokens, gate_weights.reshape(both, width), up_weights.reshape(both, width), size_x
    )
    terms = trade(terms.reshape(size_x, -1, 2 * both), "x")
    terms = jnp.sum(terms.astype(f32), axis=0).astype(bf16)
    terms = trade(terms.reshape(size_zh, -1, 2 * both), "zh")
    sums = jnp.sum(terms.astype(f32), axis=0) * scale_in
    gate_sum, up_sum = sums[:, :both], sums[:, both:]
    hidden_share = (gate_sum * jax.nn.sigmoid(gate_sum) * up_sum).astype(bf16)
    share = hidden_share.shape[0]
    hidden_rows = trade(jnp.broadcast_to(hidden_share[None], (size_zh, share, both)), "zh")
    hidden_rows = hidden_rows.reshape(size_zh * share, both)
    out_parts = jnp.stack([hidden_rows[:, :unit_count], hidden_rows[:, unit_count:]])
    out_parts = jnp.broadcast_to(out_parts[:, None], (size_c, size_x) + out_parts.shape[1:])
    hidden = trade(out_parts.reshape((size_c * size_x,) + out_parts.shape[2:]), ("c", "x"))
    hidden = hidden.reshape(size_c, token_count, unit_count)
    hidden_own = lax.dynamic_index_in_dim(hidden, core, 0, False)
    hidden_other = lax.dynamic_index_in_dim(hidden, 1 - core, 0, False)

    partial = jnp.dot(hidden_own, weights_own, preferred_element_type=f32) + jnp.dot(
        hidden_other, weights_other, preferred_element_type=f32
    )
    chips = size_y * size_zl
    rows_share = token_count // chips
    partial = trade(partial.astype(bf16).reshape(chips, rows_share, width), ("y", "zl"))
    out_share = jnp.sum(partial.astype(f32), axis=0) * scale_out
    first_row = (lax.axis_index("y") * size_zl + lax.axis_index("zl")) * rows_share
    goal = lax.dynamic_slice_in_dim(targets, first_row, rows_share, 0).astype(f32)
    d_share = (error_gain * (out_share - goal)).astype(bf16)
    d_out = trade(jnp.broadcast_to(d_share[None], (chips, rows_share, width)), ("y", "zl"))
    d_out = d_out.reshape(token_count, width)

    def grad(hidden_part):
        return jnp.dot(hidden_part.T, d_out, preferred_element_type=f32) * scale_out

    grad_other = lax.ppermute(grad(hidden_other), "c", SWAP)
    grad_own = grad(hidden_own)
    noise_own = lax.dynamic_index_in_dim(noise, core, 0, False).astype(f32)
    noise_other = lax.dynamic_index_in_dim(noise, 1 - core, 0, False).astype(f32)
    grad_mean = 0.5 * (grad_own + grad_other)
    curv_mean = 0.5 * (grad_own * noise_own + grad_other * noise_other) * inv_sigma
    new_momentum = beta_one * momentum + (1.0 - beta_one) * grad_mean
    spread = hessian - curv_mean
    new_hessian = (
        beta_two * hessian
        + (1.0 - beta_two) * curv_mean
        + 0.5 * (1.0 - beta_two) ** 2 * spread * spread / (hessian + weight_decay)
    )
    new_means = means - step_rate * (new_momentum + weight_decay * means) / (
        new_hessian + weight_decay
    )
    return (new_means, new_hessian, new_momentum)


def solution(mesh):
    fine = Mesh(mesh.devices.reshape(8, 3, 2, 4, 4), ("y", "zl", "c", "zh", "x"))
    dp, fsdp = ("y", "zl", "c"), ("zh", "x")
    in_specs = (
        P(None, fsdp),
        P(None, fsdp),
        P(None, dp, fsdp),
        P(None, dp, fsdp),
        P(dp, fsdp),
        P(dp, fsdp),
        P(dp, fsdp),
        P(None, dp, fsdp),
    )
    out_specs = (P(dp, fsdp), P(dp, fsdp), P(dp, fsdp))
    return jax.shard_map(shards, mesh=fine, in_specs=in_specs, out_specs=out_specs, check_vma=False)
```

```python
import math

import jax
import jax.numpy as jnp
from jax import lax
from jax.experimental import pallas as pl
from jax.experimental.pallas import tpu as pltpu
from jax.sharding import Mesh, PartitionSpec as P

D = 8192


prior_size = 16.0
weight_decay = 0.001
beta_one = 0.9
beta_two = 0.95
step_rate = 0.2
loss_gain = 300.0

bf16 = jnp.bfloat16
f32 = jnp.float32
SHAPE = (8, 3, 2, 4, 4)
SWAP = [(0, 1), (1, 0)]


def trade(parts, axis):
    return lax.all_to_all(parts, axis, 0, 0, tiled=True)


def turn(size, steps):
    return [(i, (i + steps) % size) for i in range(size)]


def terms_kernel(tokens_ref, gate_ref, up_ref, terms_ref):
    rows = tokens_ref[...]
    both = gate_ref.shape[0]
    for place, weights_ref in ((0, gate_ref), (both, up_ref)):
        terms_ref[:, place : place + both] = lax.dot_general(
            rows, weights_ref[...], (((1,), (1,)), ((), ())), preferred_element_type=f32
        ).astype(bf16)


def gate_up_terms(tokens, gate_weights, up_weights, blocks):
    count, width = tokens.shape
    both = gate_weights.shape[0]
    return pl.pallas_call(
        terms_kernel,
        grid=(blocks,),
        in_specs=[
            pl.BlockSpec((count // blocks, width), lambda i: (i, 0)),
            pl.BlockSpec((both, width), lambda i: (0, 0)),
            pl.BlockSpec((both, width), lambda i: (0, 0)),
        ],
        out_specs=pl.BlockSpec((count // blocks, 2 * both), lambda i: (i, 0)),
        out_shape=jax.ShapeDtypeStruct((count, 2 * both), bf16),
        compiler_params=pltpu.CompilerParams(vmem_limit_bytes=56 * 1024 * 1024),
    )(tokens, gate_weights, up_weights)


def shards(tokens, targets, gate_weights, up_weights, means, hessian, momentum, noise):
    token_count = tokens.shape[0]
    width = tokens.shape[1]
    unit_count = means.shape[0]
    size_x, size_zh = lax.axis_size("x"), lax.axis_size("zh")
    size_y, size_zl, size_c = lax.axis_size("y"), lax.axis_size("zl"), lax.axis_size("c")
    hidden_count = unit_count * size_y * size_zl * size_c
    scale_in = 1.0 / math.sqrt(D)
    scale_out = 1.0 / math.sqrt(hidden_count)
    error_gain = loss_gain / math.sqrt(token_count)
    both = 2 * unit_count
    core = lax.axis_index("c")

    terms = gate_up_terms(
        tokens, gate_weights.reshape(both, width), up_weights.reshape(both, width), size_x
    )
    terms = trade(terms.reshape(size_x, -1, 2 * both), "x")
    terms = jnp.sum(terms.astype(f32), axis=0).astype(bf16)

    inv_sigma = jnp.sqrt(prior_size * (hessian + weight_decay))
    samples = (means[None] + noise.astype(f32) / inv_sigma[None]).astype(bf16)
    weights_own = lax.dynamic_index_in_dim(samples, core, 0, False)
    weights_other = lax.ppermute(lax.dynamic_index_in_dim(samples, 1 - core, 0, False), "c", SWAP)
    weights = jnp.concatenate([weights_own, weights_other], axis=0)
    terms, weights = lax.optimization_barrier((terms, weights))
    wide = jnp.concatenate([weights] + [lax.ppermute(weights, "x", turn(size_x, k)) for k in range(1, size_x)], axis=1)

    terms = trade(terms.reshape(size_zh, -1, 2 * both), "zh")
    sums = jnp.sum(terms.astype(f32), axis=0) * scale_in
    gate_sum, up_sum = sums[:, :both], sums[:, both:]
    hidden_share = (gate_sum * jax.nn.sigmoid(gate_sum) * up_sum).astype(bf16)
    share = hidden_share.shape[0]
    parts = jnp.stack([hidden_share[:, :unit_count], hidden_share[:, unit_count:]])
    parts = jnp.broadcast_to(parts[:, None], (size_c, size_zh, share, unit_count))
    hidden = trade(parts.reshape(-1, share, unit_count), ("c", "zh"))
    rows_x = size_zh * share
    hidden = hidden.reshape(size_c, rows_x, unit_count)
    hidden_own = lax.dynamic_index_in_dim(hidden, core, 0, False)
    hidden_other = lax.dynamic_index_in_dim(hidden, 1 - core, 0, False)

    partial = jnp.dot(hidden_own, wide[:unit_count], preferred_element_type=f32) + jnp.dot(
        hidden_other, wide[unit_count:], preferred_element_type=f32
    )
    chips = size_y * size_zl
    rows_share = rows_x // chips
    partial = partial.astype(bf16).reshape(chips, rows_share, size_x * width)
    hidden, partial = lax.optimization_barrier((hidden, partial))
    here = lax.axis_index("x")
    rows = jnp.zeros((size_c, size_x, rows_x, unit_count), bf16)
    for k in range(size_x):
        block = hidden if k == 0 else lax.ppermute(hidden, "x", turn(size_x, k))
        rows = lax.dynamic_update_slice(rows, block[:, None], (0, (here - k) % size_x, 0, 0))
    rows = rows.reshape(size_c, token_count, unit_count)
    rows_own = lax.dynamic_index_in_dim(rows, core, 0, False)
    rows_other = lax.dynamic_index_in_dim(rows, 1 - core, 0, False)

    partial, rows_own, rows_other = lax.optimization_barrier(
        (trade(partial, ("y", "zl")), rows_own, rows_other)
    )
    out_share = (jnp.sum(partial.astype(f32), axis=0) * scale_out).astype(bf16)
    out_share = out_share.reshape(rows_share, size_x, width)
    sends = jnp.stack(
        [lax.dynamic_index_in_dim(out_share, (here - place) % size_x, 1, False) for place in range(size_x)]
    )
    sends = jnp.broadcast_to(sends[:, None], (size_x, chips, rows_share, width))
    out = trade(sends.reshape(-1, rows_share, width), ("x", "y", "zl")).reshape(token_count, width)
    d_out = (error_gain * (out.astype(f32) - targets.astype(f32))).astype(bf16)

    def grad(hidden_part):
        return jnp.dot(hidden_part.T, d_out, preferred_element_type=f32) * scale_out

    grad_other = lax.ppermute(grad(rows_other), "c", SWAP)
    grad_own = grad(rows_own)
    noise_own = lax.dynamic_index_in_dim(noise, core, 0, False).astype(f32)
    noise_other = lax.dynamic_index_in_dim(noise, 1 - core, 0, False).astype(f32)
    grad_mean = 0.5 * (grad_own + grad_other)
    curv_mean = 0.5 * (grad_own * noise_own + grad_other * noise_other) * inv_sigma
    new_momentum = beta_one * momentum + (1.0 - beta_one) * grad_mean
    spread = hessian - curv_mean
    new_hessian = (
        beta_two * hessian
        + (1.0 - beta_two) * curv_mean
        + 0.5 * (1.0 - beta_two) ** 2 * spread * spread / (hessian + weight_decay)
    )
    new_means = means - step_rate * (new_momentum + weight_decay * means) / (
        new_hessian + weight_decay
    )
    return (new_means, new_hessian, new_momentum)


def solution(mesh):
    fine = Mesh(mesh.devices.reshape(SHAPE), ("y", "zl", "c", "zh", "x"))
    dp, fsdp = ("y", "zl", "c"), ("zh", "x")
    in_specs = (
        P(None, fsdp),
        P(None, fsdp),
        P(None, dp, fsdp),
        P(None, dp, fsdp),
        P(dp, fsdp),
        P(dp, fsdp),
        P(dp, fsdp),
        P(None, dp, fsdp),
    )
    out_specs = (P(dp, fsdp), P(dp, fsdp), P(dp, fsdp))
    return jax.shard_map(shards, mesh=fine, in_specs=in_specs, out_specs=out_specs, check_vma=False)
```

```python
import math

import jax
import jax.numpy as jnp
from jax import lax
from jax.experimental import pallas as pl
from jax.experimental.pallas import tpu as pltpu
from jax.sharding import Mesh, PartitionSpec as P

D = 8192


prior_size = 16.0
weight_decay = 0.001
beta_one = 0.9
beta_two = 0.95
step_rate = 0.2
loss_gain = 300.0

bf16 = jnp.bfloat16
f32 = jnp.float32
SHAPE = (8, 3, 2, 4, 4)
SWAP = [(0, 1), (1, 0)]


def trade(parts, axis):
    return lax.all_to_all(parts, axis, 0, 0, tiled=True)


def turn(size, steps):
    return [(i, (i + steps) % size) for i in range(size)]


def terms_kernel(place_ref, tokens_ref, gate_ref, up_ref, earlier_ref, terms_ref):
    rows = tokens_ref[...]
    both = gate_ref.shape[0]
    for place, weights_ref in ((0, gate_ref), (both, up_ref)):
        terms_ref[:, place : place + both] = lax.dot_general(
            rows, weights_ref[...], (((1,), (1,)), ((), ())), preferred_element_type=f32
        ).astype(bf16)


def gate_up_terms(tokens, gate_weights, up_weights, rows, place, earlier):
    both, width = gate_weights.shape
    whole = pl.BlockSpec((both, width), lambda i, place: (0, 0))
    return pl.pallas_call(
        terms_kernel,
        grid_spec=pltpu.PrefetchScalarGridSpec(
            num_scalar_prefetch=1,
            grid=(1,),
            in_specs=[pl.BlockSpec((rows, width), lambda i, place: (place[0], 0)), whole, whole, pl.BlockSpec(memory_space=pl.ANY)],
            out_specs=pl.BlockSpec((rows, 2 * both), lambda i, place: (0, 0)),
        ),
        out_shape=jax.ShapeDtypeStruct((rows, 2 * both), bf16),
        cost_estimate=pl.CostEstimate(
            flops=4 * rows * both * width, bytes_accessed=2 * rows * (width + 2 * both), transcendentals=0
        ),
        compiler_params=pltpu.CompilerParams(vmem_limit_bytes=12 * 1024 * 1024),
    )(place, tokens, gate_weights, up_weights, earlier)


def first_terms_kernel(place_ref, tokens_ref, gate_ref, up_ref, terms_ref, rows, gate, up, sems):
    count = rows.shape[0]
    begin = pl.multiple_of(place_ref[0] * count, count)
    copies = [
        pltpu.make_async_copy(tokens_ref.at[pl.ds(begin, count)], rows, sems.at[0]),
        pltpu.make_async_copy(gate_ref, gate, sems.at[1]),
        pltpu.make_async_copy(up_ref, up, sems.at[2]),
    ]
    for copy in copies:
        copy.start()
    copies[0].wait()
    copies[1].wait()
    both = gate.shape[0]
    for place, weights, copy in ((0, gate, None), (both, up, copies[2])):
        if copy is not None:
            copy.wait()
        terms_ref[:, place : place + both] = lax.dot_general(
            rows[...], weights[...], (((1,), (1,)), ((), ())), preferred_element_type=f32
        ).astype(bf16)


def first_gate_up_terms(tokens, gate_weights, up_weights, rows, place):
    both, width = gate_weights.shape
    far = pl.BlockSpec(memory_space=pltpu.HBM)
    return pl.pallas_call(
        first_terms_kernel,
        grid_spec=pltpu.PrefetchScalarGridSpec(
            num_scalar_prefetch=1,
            grid=(1,),
            in_specs=[far, far, far],
            out_specs=pl.BlockSpec((rows, 2 * both), lambda i, place: (0, 0)),
            scratch_shapes=[
                pltpu.VMEM((rows, width), bf16),
                pltpu.VMEM((both, width), bf16),
                pltpu.VMEM((both, width), bf16),
                pltpu.SemaphoreType.DMA((3,)),
            ],
        ),
        out_shape=jax.ShapeDtypeStruct((rows, 2 * both), bf16),
        cost_estimate=pl.CostEstimate(
            flops=4 * rows * both * width, bytes_accessed=2 * rows * (width + 2 * both), transcendentals=0
        ),
        compiler_params=pltpu.CompilerParams(vmem_limit_bytes=56 * 1024 * 1024),
    )(place, tokens, gate_weights, up_weights)


def shards(tokens, targets, gate_weights, up_weights, means, hessian, momentum, noise):
    token_count = tokens.shape[0]
    width = tokens.shape[1]
    unit_count = means.shape[0]
    size_x, size_zh = lax.axis_size("x"), lax.axis_size("zh")
    size_y, size_zl, size_c = lax.axis_size("y"), lax.axis_size("zl"), lax.axis_size("c")
    hidden_count = unit_count * size_y * size_zl * size_c
    scale_in = 1.0 / math.sqrt(D)
    scale_out = 1.0 / math.sqrt(hidden_count)
    error_gain = loss_gain / math.sqrt(token_count)
    both = 2 * unit_count
    core = lax.axis_index("c")

    here = lax.axis_index("x")
    gate_both, up_both = gate_weights.reshape(both, width), up_weights.reshape(both, width)

    order = sorted(range(1, size_x), key=lambda k: -min(k, size_x - k)) + [0]
    block, terms = None, 0.0
    for k in order:
        rows = (tokens, gate_both, up_both, token_count // size_x)
        place = jnp.full((1,), (here + k) % size_x, jnp.int32)
        if block is None:
            block = first_gate_up_terms(*rows, place)
        else:
            block = gate_up_terms(*rows, place, block)
        arrived = lax.ppermute(block, "x", turn(size_x, k)) if k else block
        terms = terms + arrived.astype(f32)
    terms = terms.astype(bf16)

    inv_sigma = jnp.sqrt(prior_size * (hessian + weight_decay))
    samples = (means[None] + noise.astype(f32) / inv_sigma[None]).astype(bf16)
    weights_own = lax.dynamic_index_in_dim(samples, core, 0, False)
    weights_other = lax.ppermute(lax.dynamic_index_in_dim(samples, 1 - core, 0, False), "c", SWAP)
    weights = jnp.concatenate([weights_own, weights_other], axis=0)
    terms, weights = lax.optimization_barrier((terms, weights))
    wide = jnp.concatenate([weights] + [lax.ppermute(weights, "x", turn(size_x, k)) for k in range(1, size_x)], axis=1)

    terms = trade(terms.reshape(size_zh, -1, 2 * both), "zh")
    sums = jnp.sum(terms.astype(f32), axis=0) * scale_in
    gate_sum, up_sum = sums[:, :both], sums[:, both:]
    hidden_share = (gate_sum * jax.nn.sigmoid(gate_sum) * up_sum).astype(bf16)
    share = hidden_share.shape[0]
    parts = jnp.stack([hidden_share[:, :unit_count], hidden_share[:, unit_count:]])
    parts = jnp.broadcast_to(parts[:, None], (size_c, size_zh, share, unit_count))
    hidden = trade(parts.reshape(-1, share, unit_count), ("c", "zh"))
    rows_x = size_zh * share
    hidden = hidden.reshape(size_c, rows_x, unit_count)
    hidden_own = lax.dynamic_index_in_dim(hidden, core, 0, False)
    hidden_other = lax.dynamic_index_in_dim(hidden, 1 - core, 0, False)

    partial = jnp.dot(hidden_own, wide[:unit_count], preferred_element_type=f32) + jnp.dot(
        hidden_other, wide[unit_count:], preferred_element_type=f32
    )
    chips = size_y * size_zl
    rows_share = rows_x // chips
    partial = partial.astype(bf16).reshape(chips, rows_share, size_x * width)
    hidden, partial = lax.optimization_barrier((hidden, partial))
    rows = jnp.zeros((size_c, size_x, rows_x, unit_count), bf16)
    for k in range(size_x):
        block = hidden if k == 0 else lax.ppermute(hidden, "x", turn(size_x, k))
        rows = lax.dynamic_update_slice(rows, block[:, None], (0, (here - k) % size_x, 0, 0))
    rows = rows.reshape(size_c, token_count, unit_count)
    rows_own = lax.dynamic_index_in_dim(rows, core, 0, False)
    rows_other = lax.dynamic_index_in_dim(rows, 1 - core, 0, False)

    partial, rows_own, rows_other = lax.optimization_barrier(
        (trade(partial, ("y", "zl")), rows_own, rows_other)
    )
    out_share = (jnp.sum(partial.astype(f32), axis=0) * scale_out).astype(bf16)
    out_share = out_share.reshape(rows_share, size_x, width)
    sends = jnp.stack(
        [lax.dynamic_index_in_dim(out_share, (here - place) % size_x, 1, False) for place in range(size_x)]
    )
    sends = jnp.broadcast_to(sends[:, None], (size_x, chips, rows_share, width))
    out = trade(sends.reshape(-1, rows_share, width), ("x", "y", "zl")).reshape(token_count, width)
    d_out = (error_gain * (out.astype(f32) - targets.astype(f32))).astype(bf16)

    def grad(hidden_part):
        return jnp.dot(hidden_part.T, d_out, preferred_element_type=f32) * scale_out

    grad_other = lax.ppermute(grad(rows_other), "c", SWAP)
    grad_own = grad(rows_own)
    noise_own = lax.dynamic_index_in_dim(noise, core, 0, False).astype(f32)
    noise_other = lax.dynamic_index_in_dim(noise, 1 - core, 0, False).astype(f32)
    grad_mean = 0.5 * (grad_own + grad_other)
    curv_mean = 0.5 * (grad_own * noise_own + grad_other * noise_other) * inv_sigma
    new_momentum = beta_one * momentum + (1.0 - beta_one) * grad_mean
    spread = hessian - curv_mean
    new_hessian = (
        beta_two * hessian
        + (1.0 - beta_two) * curv_mean
        + 0.5 * (1.0 - beta_two) ** 2 * spread * spread / (hessian + weight_decay)
    )
    new_means = means - step_rate * (new_momentum + weight_decay * means) / (
        new_hessian + weight_decay
    )
    return (new_means, new_hessian, new_momentum)


def solution(mesh):
    fine = Mesh(mesh.devices.reshape(SHAPE), ("y", "zl", "c", "zh", "x"))
    dp, fsdp = ("y", "zl", "c"), ("zh", "x")
    in_specs = (
        P(None, fsdp),
        P(None, fsdp),
        P(None, dp, fsdp),
        P(None, dp, fsdp),
        P(dp, fsdp),
        P(dp, fsdp),
        P(dp, fsdp),
        P(None, dp, fsdp),
    )
    out_specs = (P(dp, fsdp), P(dp, fsdp), P(dp, fsdp))
    return jax.shard_map(shards, mesh=fine, in_specs=in_specs, out_specs=out_specs, check_vma=False)
```

```python
import math

import jax
import jax.numpy as jnp
from jax import lax
from jax.experimental import pallas as pl
from jax.experimental.pallas import tpu as pltpu
from jax.sharding import Mesh, PartitionSpec as P

D = 8192


prior_size = 16.0
weight_decay = 0.001
beta_one = 0.9
beta_two = 0.95
step_rate = 0.2
loss_gain = 300.0

bf16 = jnp.bfloat16
f32 = jnp.float32
SHAPE = (8, 3, 2, 4, 4)
SWAP = [(0, 1), (1, 0)]


def trade(parts, axis):
    return lax.all_to_all(parts, axis, 0, 0, tiled=True)


def turn(size, steps):
    return [(i, (i + steps) % size) for i in range(size)]


def terms_kernel(tokens_ref, gate_ref, up_ref, terms_ref):
    rows = tokens_ref[...]
    both = gate_ref.shape[0]
    for place, weights_ref in ((0, gate_ref), (both, up_ref)):
        terms_ref[:, place : place + both] = lax.dot_general(
            rows, weights_ref[...], (((1,), (1,)), ((), ())), preferred_element_type=f32
        ).astype(bf16)


def gate_up_terms(tokens, gate_weights, up_weights, blocks):
    count, width = tokens.shape
    both = gate_weights.shape[0]
    return pl.pallas_call(
        terms_kernel,
        grid=(blocks,),
        in_specs=[
            pl.BlockSpec((count // blocks, width), lambda i: (i, 0)),
            pl.BlockSpec((both, width), lambda i: (0, 0)),
            pl.BlockSpec((both, width), lambda i: (0, 0)),
        ],
        out_specs=pl.BlockSpec((count // blocks, 2 * both), lambda i: (i, 0)),
        out_shape=jax.ShapeDtypeStruct((count, 2 * both), bf16),
        compiler_params=pltpu.CompilerParams(vmem_limit_bytes=56 * 1024 * 1024),
    )(tokens, gate_weights, up_weights)


def shards(tokens, targets, gate_weights, up_weights, means, hessian, momentum, noise):
    token_count = tokens.shape[0]
    width = tokens.shape[1]
    unit_count = means.shape[0]
    size_x, size_zh = lax.axis_size("x"), lax.axis_size("zh")
    size_y, size_zl, size_c = lax.axis_size("y"), lax.axis_size("zl"), lax.axis_size("c")
    hidden_count = unit_count * size_y * size_zl * size_c
    scale_in = 1.0 / math.sqrt(D)
    scale_out = 1.0 / math.sqrt(hidden_count)
    error_gain = loss_gain / math.sqrt(token_count)
    both = 2 * unit_count
    core = lax.axis_index("c")

    terms = gate_up_terms(
        tokens, gate_weights.reshape(both, width), up_weights.reshape(both, width), 2
    )
    terms = trade(terms.reshape(size_x, -1, 2 * both), "x")
    terms = jnp.sum(terms.astype(f32), axis=0).astype(bf16)

    inv_sigma = jnp.sqrt(prior_size * (hessian + weight_decay))
    samples = (means[None] + noise.astype(f32) / inv_sigma[None]).astype(bf16)
    weights_own = lax.dynamic_index_in_dim(samples, core, 0, False)
    weights_other = lax.ppermute(lax.dynamic_index_in_dim(samples, 1 - core, 0, False), "c", SWAP)
    weights = jnp.concatenate([weights_own, weights_other], axis=0)
    terms, weights = lax.optimization_barrier((terms, weights))
    wide = jnp.concatenate([weights] + [lax.ppermute(weights, "x", turn(size_x, k)) for k in range(1, size_x)], axis=1)

    terms = trade(terms.reshape(size_zh, -1, 2 * both), "zh")
    sums = jnp.sum(terms.astype(f32), axis=0) * scale_in
    gate_sum, up_sum = sums[:, :both], sums[:, both:]
    hidden_share = (gate_sum * jax.nn.sigmoid(gate_sum) * up_sum).astype(bf16)
    share = hidden_share.shape[0]
    parts = jnp.stack([hidden_share[:, :unit_count], hidden_share[:, unit_count:]])
    parts = jnp.broadcast_to(parts[:, None], (size_c, size_zh, share, unit_count))
    hidden = trade(parts.reshape(-1, share, unit_count), ("c", "zh"))
    rows_x = size_zh * share
    hidden = hidden.reshape(size_c, rows_x, unit_count)
    hidden_own = lax.dynamic_index_in_dim(hidden, core, 0, False)
    hidden_other = lax.dynamic_index_in_dim(hidden, 1 - core, 0, False)

    partial = jnp.dot(hidden_own, wide[:unit_count], preferred_element_type=f32) + jnp.dot(
        hidden_other, wide[unit_count:], preferred_element_type=f32
    )
    chips = size_y * size_zl
    rows_share = rows_x // chips
    partial = partial.astype(bf16).reshape(chips, rows_share, size_x * width)
    hidden, partial = lax.optimization_barrier((hidden, partial))
    here = lax.axis_index("x")
    near = {k: lax.ppermute(hidden, "x", turn(size_x, k)) for k in (1, size_x - 1)}
    partial, near = lax.optimization_barrier((trade(partial, ("y", "zl")), near))
    out_share = (jnp.sum(partial.astype(f32), axis=0) * scale_out).astype(bf16)
    out_share = out_share.reshape(rows_share, size_x, width)
    out_share, hidden = lax.optimization_barrier((out_share, hidden))
    rows = jnp.zeros((size_c, size_x, rows_x, unit_count), bf16)
    for k in range(size_x):
        block = near.get(k, hidden)
        if k and k not in near:
            block = lax.ppermute(hidden, "x", turn(size_x, k))
        rows = lax.dynamic_update_slice(rows, block[:, None], (0, (here - k) % size_x, 0, 0))
    rows = rows.reshape(size_c, token_count, unit_count)
    rows_own = lax.dynamic_index_in_dim(rows, core, 0, False)
    rows_other = lax.dynamic_index_in_dim(rows, 1 - core, 0, False)
    sends = jnp.stack(
        [lax.dynamic_index_in_dim(out_share, (here - place) % size_x, 1, False) for place in range(size_x)]
    )
    sends = jnp.broadcast_to(sends[:, None], (size_x, chips, rows_share, width))
    out = trade(sends.reshape(-1, rows_share, width), ("x", "y", "zl")).reshape(token_count, width)
    d_out = (error_gain * (out.astype(f32) - targets.astype(f32))).astype(bf16)

    def grad(hidden_part):
        return jnp.dot(hidden_part.T, d_out, preferred_element_type=f32) * scale_out

    grad_other = lax.ppermute(grad(rows_other), "c", SWAP)
    grad_own = grad(rows_own)
    noise_own = lax.dynamic_index_in_dim(noise, core, 0, False).astype(f32)
    noise_other = lax.dynamic_index_in_dim(noise, 1 - core, 0, False).astype(f32)
    grad_mean = 0.5 * (grad_own + grad_other)
    curv_mean = 0.5 * (grad_own * noise_own + grad_other * noise_other) * inv_sigma
    new_momentum = beta_one * momentum + (1.0 - beta_one) * grad_mean
    spread = hessian - curv_mean
    new_hessian = (
        beta_two * hessian
        + (1.0 - beta_two) * curv_mean
        + 0.5 * (1.0 - beta_two) ** 2 * spread * spread / (hessian + weight_decay)
    )
    new_means = means - step_rate * (new_momentum + weight_decay * means) / (
        new_hessian + weight_decay
    )
    return (new_means, new_hessian, new_momentum)


def solution(mesh):
    fine = Mesh(mesh.devices.reshape(SHAPE), ("y", "zl", "c", "zh", "x"))
    dp, fsdp = ("y", "zl", "c"), ("zh", "x")
    in_specs = (
        P(None, fsdp),
        P(None, fsdp),
        P(None, dp, fsdp),
        P(None, dp, fsdp),
        P(dp, fsdp),
        P(dp, fsdp),
        P(dp, fsdp),
        P(None, dp, fsdp),
    )
    out_specs = (P(dp, fsdp), P(dp, fsdp), P(dp, fsdp))
    return jax.shard_map(shards, mesh=fine, in_specs=in_specs, out_specs=out_specs, check_vma=False)
```

```python
import math

import jax
import jax.numpy as jnp
from jax import lax
from jax.experimental import pallas as pl
from jax.experimental.pallas import tpu as pltpu
from jax.sharding import Mesh, PartitionSpec as P

D = 8192


prior_size = 16.0
weight_decay = 0.001
beta_one = 0.9
beta_two = 0.95
step_rate = 0.2
loss_gain = 300.0

bf16 = jnp.bfloat16
f32 = jnp.float32
SHAPE = (8, 3, 2, 4, 4)
SWAP = [(0, 1), (1, 0)]


def trade(parts, axis):
    return lax.all_to_all(parts, axis, 0, 0, tiled=True)


def turn(size, steps):
    return [(i, (i + steps) % size) for i in range(size)]


def terms_kernel(tokens_ref, gate_ref, up_ref, terms_ref):
    rows = tokens_ref[...]
    both = gate_ref.shape[0]
    for place, weights_ref in ((0, gate_ref), (both, up_ref)):
        terms_ref[:, place : place + both] = lax.dot_general(
            rows, weights_ref[...], (((1,), (1,)), ((), ())), preferred_element_type=f32
        ).astype(bf16)


def gate_up_terms(tokens, gate_weights, up_weights, blocks):
    count, width = tokens.shape
    both = gate_weights.shape[0]
    return pl.pallas_call(
        terms_kernel,
        grid=(blocks,),
        in_specs=[
            pl.BlockSpec((count // blocks, width), lambda i: (i, 0)),
            pl.BlockSpec((both, width), lambda i: (0, 0)),
            pl.BlockSpec((both, width), lambda i: (0, 0)),
        ],
        out_specs=pl.BlockSpec((count // blocks, 2 * both), lambda i: (i, 0)),
        out_shape=jax.ShapeDtypeStruct((count, 2 * both), bf16),
        compiler_params=pltpu.CompilerParams(vmem_limit_bytes=56 * 1024 * 1024),
    )(tokens, gate_weights, up_weights)


def shards(tokens, targets, gate_weights, up_weights, means, hessian, momentum, noise):
    token_count = tokens.shape[0]
    width = tokens.shape[1]
    unit_count = means.shape[0]
    size_x, size_zh = lax.axis_size("x"), lax.axis_size("zh")
    size_y, size_zl, size_c = lax.axis_size("y"), lax.axis_size("zl"), lax.axis_size("c")
    hidden_count = unit_count * size_y * size_zl * size_c
    scale_in = 1.0 / math.sqrt(D)
    scale_out = 1.0 / math.sqrt(hidden_count)
    error_gain = loss_gain / math.sqrt(token_count)
    both = 2 * unit_count
    core = lax.axis_index("c")

    terms = gate_up_terms(
        tokens, gate_weights.reshape(both, width), up_weights.reshape(both, width), 2
    )
    terms = trade(terms.reshape(size_x, -1, 2 * both), "x")
    terms = jnp.sum(terms.astype(f32), axis=0).astype(bf16)

    inv_sigma = jnp.sqrt(prior_size * (hessian + weight_decay))
    samples = (means[None] + noise.astype(f32) / inv_sigma[None]).astype(bf16)
    weights_own = lax.dynamic_index_in_dim(samples, core, 0, False)
    weights_other = lax.ppermute(lax.dynamic_index_in_dim(samples, 1 - core, 0, False), "c", SWAP)
    weights = jnp.concatenate([weights_own, weights_other], axis=0)
    terms, weights = lax.optimization_barrier((terms, weights))
    wide = jnp.concatenate([weights] + [lax.ppermute(weights, "x", turn(size_x, k)) for k in range(1, size_x)], axis=1)

    terms = trade(terms.reshape(size_zh, -1, 2 * both), "zh")
    sums = jnp.sum(terms.astype(f32), axis=0) * scale_in
    gate_sum, up_sum = sums[:, :both], sums[:, both:]
    hidden_share = (gate_sum * jax.nn.sigmoid(gate_sum) * up_sum).astype(bf16)
    share = hidden_share.shape[0]
    parts = jnp.stack([hidden_share[:, :unit_count], hidden_share[:, unit_count:]])
    parts = jnp.broadcast_to(parts[:, None], (size_c, size_zh, share, unit_count))
    hidden = trade(parts.reshape(-1, share, unit_count), ("c", "zh"))
    rows_x = size_zh * share
    hidden = hidden.reshape(size_c, rows_x, unit_count)
    hidden_own = lax.dynamic_index_in_dim(hidden, core, 0, False)
    hidden_other = lax.dynamic_index_in_dim(hidden, 1 - core, 0, False)

    partial = jnp.dot(hidden_own, wide[:unit_count], preferred_element_type=f32) + jnp.dot(
        hidden_other, wide[unit_count:], preferred_element_type=f32
    )
    chips = size_y * size_zl
    rows_share = rows_x // chips
    partial = partial.astype(bf16).reshape(chips, rows_share, size_x * width)
    hidden, partial = lax.optimization_barrier((hidden, partial))
    here = lax.axis_index("x")
    rows = jnp.zeros((size_c, size_x, rows_x, unit_count), bf16)
    for k in range(size_x):
        block = hidden if k == 0 else lax.ppermute(hidden, "x", turn(size_x, k))
        rows = lax.dynamic_update_slice(rows, block[:, None], (0, (here - k) % size_x, 0, 0))
    rows = rows.reshape(size_c, token_count, unit_count)
    rows_own = lax.dynamic_index_in_dim(rows, core, 0, False)
    rows_other = lax.dynamic_index_in_dim(rows, 1 - core, 0, False)

    partial, rows_own, rows_other = lax.optimization_barrier(
        (trade(partial, ("y", "zl")), rows_own, rows_other)
    )
    out_share = (jnp.sum(partial.astype(f32), axis=0) * scale_out).astype(bf16)
    out_share = out_share.reshape(rows_share, size_x, width)
    sends = jnp.stack(
        [lax.dynamic_index_in_dim(out_share, (here - place) % size_x, 1, False) for place in range(size_x)]
    )
    sends = jnp.broadcast_to(sends[:, None], (size_x, chips, rows_share, width))
    out = trade(sends.reshape(-1, rows_share, width), ("x", "y", "zl")).reshape(token_count, width)
    d_out = (error_gain * (out.astype(f32) - targets.astype(f32))).astype(bf16)

    def grad(hidden_part):
        return jnp.dot(hidden_part.T, d_out, preferred_element_type=f32) * scale_out

    grad_sent = grad(rows_other)
    grad_own = grad(rows_own)
    noise_own = lax.dynamic_index_in_dim(noise, core, 0, False).astype(f32)
    noise_other = lax.dynamic_index_in_dim(noise, 1 - core, 0, False).astype(f32) * (0.5 * inv_sigma)
    momentum_own = beta_one * momentum + (1.0 - beta_one) * 0.5 * grad_own
    curv_own = grad_own * noise_own * (0.5 * inv_sigma)
    spread_gain = 0.5 * (1.0 - beta_two) ** 2 / (hessian + weight_decay)
    grad_other, momentum_own, curv_own, noise_other, spread_gain = lax.optimization_barrier(
        (lax.ppermute(grad_sent, "c", SWAP), momentum_own, curv_own, noise_other, spread_gain)
    )
    new_momentum = momentum_own + (1.0 - beta_one) * 0.5 * grad_other
    curv_mean = curv_own + grad_other * noise_other
    spread = hessian - curv_mean
    new_hessian = beta_two * hessian + (1.0 - beta_two) * curv_mean + spread_gain * spread * spread
    new_means = means - step_rate * (new_momentum + weight_decay * means) / (
        new_hessian + weight_decay
    )
    return (new_means, new_hessian, new_momentum)


def solution(mesh):
    fine = Mesh(mesh.devices.reshape(SHAPE), ("y", "zl", "c", "zh", "x"))
    dp, fsdp = ("y", "zl", "c"), ("zh", "x")
    in_specs = (
        P(None, fsdp),
        P(None, fsdp),
        P(None, dp, fsdp),
        P(None, dp, fsdp),
        P(dp, fsdp),
        P(dp, fsdp),
        P(dp, fsdp),
        P(None, dp, fsdp),
    )
    out_specs = (P(dp, fsdp), P(dp, fsdp), P(dp, fsdp))
    return jax.shard_map(shards, mesh=fine, in_specs=in_specs, out_specs=out_specs, check_vma=False)
```

```python
import math

import jax
import jax.numpy as jnp
from jax import lax
from jax.experimental import pallas as pl
from jax.experimental.pallas import tpu as pltpu
from jax.sharding import Mesh, PartitionSpec as P

D = 8192


prior_size = 16.0
weight_decay = 0.001
beta_one = 0.9
beta_two = 0.95
step_rate = 0.2
loss_gain = 300.0

bf16 = jnp.bfloat16
f32 = jnp.float32
SHAPE = (8, 3, 2, 4, 4)
SWAP = [(0, 1), (1, 0)]


def trade(parts, axis):
    return lax.all_to_all(parts, axis, 0, 0, tiled=True)


def turn(size, steps):
    return [(i, (i + steps) % size) for i in range(size)]


def farthest_first(size):
    return sorted(range(1, size), key=lambda k: -min(k, size - k))


def terms_kernel(tokens_ref, gate_ref, up_ref, terms_ref):
    rows = tokens_ref[...]
    both = gate_ref.shape[0]
    for place, weights_ref in ((0, gate_ref), (both, up_ref)):
        terms_ref[:, place : place + both] = lax.dot_general(
            rows, weights_ref[...], (((1,), (1,)), ((), ())), preferred_element_type=f32
        ).astype(bf16)


def gate_up_terms(tokens, gate_weights, up_weights, blocks):
    count, width = tokens.shape
    both = gate_weights.shape[0]
    return pl.pallas_call(
        terms_kernel,
        grid=(blocks,),
        in_specs=[
            pl.BlockSpec((count // blocks, width), lambda i: (i, 0)),
            pl.BlockSpec((both, width), lambda i: (0, 0)),
            pl.BlockSpec((both, width), lambda i: (0, 0)),
        ],
        out_specs=pl.BlockSpec((count // blocks, 2 * both), lambda i: (i, 0)),
        out_shape=jax.ShapeDtypeStruct((count, 2 * both), bf16),
        compiler_params=pltpu.CompilerParams(vmem_limit_bytes=56 * 1024 * 1024),
    )(tokens, gate_weights, up_weights)


def shards(tokens, targets, gate_weights, up_weights, means, hessian, momentum, noise):
    token_count = tokens.shape[0]
    width = tokens.shape[1]
    unit_count = means.shape[0]
    size_x, size_zh = lax.axis_size("x"), lax.axis_size("zh")
    size_y, size_zl, size_c = lax.axis_size("y"), lax.axis_size("zl"), lax.axis_size("c")
    hidden_count = unit_count * size_y * size_zl * size_c
    scale_in = 1.0 / math.sqrt(D)
    scale_out = 1.0 / math.sqrt(hidden_count)
    error_gain = loss_gain / math.sqrt(token_count)
    both = 2 * unit_count
    core = lax.axis_index("c")

    terms = gate_up_terms(
        tokens, gate_weights.reshape(both, width), up_weights.reshape(both, width), 2
    )
    terms = trade(terms.reshape(size_x, -1, 2 * both), "x")
    terms = jnp.sum(terms.astype(f32), axis=0).astype(bf16)

    inv_sigma = jnp.sqrt(prior_size * (hessian + weight_decay))
    samples = (means[None] + noise.astype(f32) / inv_sigma[None]).astype(bf16)
    weights_own = lax.dynamic_index_in_dim(samples, core, 0, False)
    weights_other = lax.ppermute(lax.dynamic_index_in_dim(samples, 1 - core, 0, False), "c", SWAP)
    weights = jnp.concatenate([weights_own, weights_other], axis=0)
    terms, weights = lax.optimization_barrier((terms, weights))
    slots = [0] + farthest_first(size_x)
    wide = jnp.concatenate(
        [lax.ppermute(weights, "x", turn(size_x, k)) if k else weights for k in slots], axis=1
    )

    terms = trade(terms.reshape(size_zh, -1, 2 * both), "zh")
    sums = jnp.sum(terms.astype(f32), axis=0) * scale_in
    gate_sum, up_sum = sums[:, :both], sums[:, both:]
    hidden_share = (gate_sum * jax.nn.sigmoid(gate_sum) * up_sum).astype(bf16)
    share = hidden_share.shape[0]
    parts = jnp.stack([hidden_share[:, :unit_count], hidden_share[:, unit_count:]])
    parts = jnp.broadcast_to(parts[:, None], (size_c, size_zh, share, unit_count))
    hidden = trade(parts.reshape(-1, share, unit_count), ("c", "zh"))
    rows_x = size_zh * share
    hidden = hidden.reshape(size_c, rows_x, unit_count)
    hidden_own = lax.dynamic_index_in_dim(hidden, core, 0, False)
    hidden_other = lax.dynamic_index_in_dim(hidden, 1 - core, 0, False)

    partial = jnp.dot(hidden_own, wide[:unit_count], preferred_element_type=f32) + jnp.dot(
        hidden_other, wide[unit_count:], preferred_element_type=f32
    )
    chips = size_y * size_zl
    rows_share = rows_x // chips
    partial = partial.astype(bf16).reshape(chips, rows_share, size_x * width)
    hidden, partial = lax.optimization_barrier((hidden, partial))
    here = lax.axis_index("x")
    rows = jnp.zeros((size_c, size_x, rows_x, unit_count), bf16)
    for k in range(size_x):
        block = hidden if k == 0 else lax.ppermute(hidden, "x", turn(size_x, k))
        rows = lax.dynamic_update_slice(rows, block[:, None], (0, (here - k) % size_x, 0, 0))
    rows = rows.reshape(size_c, token_count, unit_count)
    rows_own = lax.dynamic_index_in_dim(rows, core, 0, False)
    rows_other = lax.dynamic_index_in_dim(rows, 1 - core, 0, False)

    partial, rows_own, rows_other = lax.optimization_barrier(
        (trade(partial, ("y", "zl")), rows_own, rows_other)
    )
    out_share = (jnp.sum(partial.astype(f32), axis=0) * scale_out).astype(bf16)
    out_share = out_share.reshape(rows_share, size_x, width)
    slot_of = jnp.asarray([slots.index(k) for k in range(size_x)], jnp.int32)
    sends = jnp.stack(
        [
            lax.dynamic_index_in_dim(out_share, slot_of[(here - place) % size_x], 1, False)
            for place in range(size_x)
        ]
    )
    sends = jnp.broadcast_to(sends[:, None], (size_x, chips, rows_share, width))
    out = trade(sends.reshape(-1, rows_share, width), ("x", "y", "zl")).reshape(token_count, width)
    d_out = (error_gain * (out.astype(f32) - targets.astype(f32))).astype(bf16)

    def grad(hidden_part):
        return jnp.dot(hidden_part.T, d_out, preferred_element_type=f32) * scale_out

    grad_sent = grad(rows_other)
    grad_own = grad(rows_own)
    noise_own = lax.dynamic_index_in_dim(noise, core, 0, False).astype(f32)
    noise_other = lax.dynamic_index_in_dim(noise, 1 - core, 0, False).astype(f32) * (0.5 * inv_sigma)
    momentum_own = beta_one * momentum + (1.0 - beta_one) * 0.5 * grad_own
    curv_own = grad_own * noise_own * (0.5 * inv_sigma)
    spread_gain = 0.5 * (1.0 - beta_two) ** 2 / (hessian + weight_decay)
    grad_other, momentum_own, curv_own, noise_other, spread_gain = lax.optimization_barrier(
        (lax.ppermute(grad_sent.astype(bf16), "c", SWAP), momentum_own, curv_own, noise_other, spread_gain)
    )
    grad_other = grad_other.astype(f32)
    new_momentum = momentum_own + (1.0 - beta_one) * 0.5 * grad_other
    curv_mean = curv_own + grad_other * noise_other
    spread = hessian - curv_mean
    new_hessian = beta_two * hessian + (1.0 - beta_two) * curv_mean + spread_gain * spread * spread
    new_means = means - step_rate * (new_momentum + weight_decay * means) / (
        new_hessian + weight_decay
    )
    return (new_means, new_hessian, new_momentum)


def solution(mesh):
    fine = Mesh(mesh.devices.reshape(SHAPE), ("y", "zl", "c", "zh", "x"))
    dp, fsdp = ("y", "zl", "c"), ("zh", "x")
    in_specs = (
        P(None, fsdp),
        P(None, fsdp),
        P(None, dp, fsdp),
        P(None, dp, fsdp),
        P(dp, fsdp),
        P(dp, fsdp),
        P(dp, fsdp),
        P(None, dp, fsdp),
    )
    out_specs = (P(dp, fsdp), P(dp, fsdp), P(dp, fsdp))
    return jax.shard_map(shards, mesh=fine, in_specs=in_specs, out_specs=out_specs, check_vma=False)
```

```python
import math

import jax
import jax.numpy as jnp
from jax import lax
from jax.experimental import pallas as pl
from jax.experimental.pallas import tpu as pltpu
from jax.sharding import Mesh, PartitionSpec as P

D = 8192


prior_size = 16.0
weight_decay = 0.001
beta_one = 0.9
beta_two = 0.95
step_rate = 0.2
loss_gain = 300.0

bf16 = jnp.bfloat16
f32 = jnp.float32
SHAPE = (8, 3, 2, 4, 4)
SWAP = [(0, 1), (1, 0)]


def trade(parts, axis):
    return lax.all_to_all(parts, axis, 0, 0, tiled=True)


def turn(size, steps):
    return [(i, (i + steps) % size) for i in range(size)]


def terms_kernel(tokens_ref, gate_ref, up_ref, terms_ref):
    rows = tokens_ref[...]
    both = gate_ref.shape[0]
    for place, weights_ref in ((0, gate_ref), (both, up_ref)):
        terms_ref[:, place : place + both] = lax.dot_general(
            rows, weights_ref[...], (((1,), (1,)), ((), ())), preferred_element_type=f32
        ).astype(bf16)


def gate_up_terms(tokens, gate_weights, up_weights, blocks):
    count, width = tokens.shape
    both = gate_weights.shape[0]
    return pl.pallas_call(
        terms_kernel,
        grid=(blocks,),
        in_specs=[
            pl.BlockSpec((count // blocks, width), lambda i: (i, 0)),
            pl.BlockSpec((both, width), lambda i: (0, 0)),
            pl.BlockSpec((both, width), lambda i: (0, 0)),
        ],
        out_specs=pl.BlockSpec((count // blocks, 2 * both), lambda i: (i, 0)),
        out_shape=jax.ShapeDtypeStruct((count, 2 * both), bf16),
        compiler_params=pltpu.CompilerParams(vmem_limit_bytes=56 * 1024 * 1024),
    )(tokens, gate_weights, up_weights)


def shards(tokens, targets, gate_weights, up_weights, means, hessian, momentum, noise):
    token_count = tokens.shape[0]
    width = tokens.shape[1]
    unit_count = means.shape[0]
    size_x, size_zh = lax.axis_size("x"), lax.axis_size("zh")
    size_y, size_zl, size_c = lax.axis_size("y"), lax.axis_size("zl"), lax.axis_size("c")
    hidden_count = unit_count * size_y * size_zl * size_c
    scale_in = 1.0 / math.sqrt(D)
    scale_out = 1.0 / math.sqrt(hidden_count)
    error_gain = loss_gain / math.sqrt(token_count)
    both = 2 * unit_count
    core = lax.axis_index("c")

    terms = gate_up_terms(
        tokens, gate_weights.reshape(both, width), up_weights.reshape(both, width), 2
    )
    terms = trade(terms.reshape(size_x, -1, 2 * both), "x")
    terms = jnp.sum(terms.astype(f32), axis=0).astype(bf16)

    inv_sigma = jnp.sqrt(prior_size * (hessian + weight_decay))
    samples = (means[None] + noise.astype(f32) / inv_sigma[None]).astype(bf16)
    weights_own = lax.dynamic_index_in_dim(samples, core, 0, False)
    weights_other = lax.ppermute(lax.dynamic_index_in_dim(samples, 1 - core, 0, False), "c", SWAP)
    weights = jnp.concatenate([weights_own, weights_other], axis=0)
    terms, weights = lax.optimization_barrier((terms, weights))
    wide = jnp.concatenate([weights] + [lax.ppermute(weights, "x", turn(size_x, k)) for k in range(1, size_x)], axis=1)

    terms = trade(terms.reshape(size_zh, -1, 2 * both), "zh")
    sums = jnp.sum(terms.astype(f32), axis=0) * scale_in
    gate_sum, up_sum = sums[:, :both], sums[:, both:]
    hidden_share = (gate_sum * jax.nn.sigmoid(gate_sum) * up_sum).astype(bf16)
    share = hidden_share.shape[0]
    parts = jnp.stack([hidden_share[:, :unit_count], hidden_share[:, unit_count:]])
    parts = jnp.broadcast_to(parts[:, None], (size_c, size_zh, share, unit_count))
    hidden = trade(parts.reshape(-1, share, unit_count), ("c", "zh"))
    rows_x = size_zh * share
    hidden = hidden.reshape(size_c, rows_x, unit_count)
    hidden = jnp.concatenate(
        [
            lax.dynamic_index_in_dim(hidden, core, 0, False),
            lax.dynamic_index_in_dim(hidden, 1 - core, 0, False),
        ],
        axis=1,
    )

    wide = lax.optimization_barrier(wide)
    partial = jnp.dot(hidden, wide, preferred_element_type=f32)
    chips = size_y * size_zl
    rows_share = rows_x // chips
    partial = partial.astype(bf16).reshape(chips, rows_share, size_x * width)
    hidden, partial = lax.optimization_barrier((hidden, partial))
    here = lax.axis_index("x")
    rows = jnp.zeros((size_x, rows_x, both), bf16)
    for k in range(size_x):
        block = hidden if k == 0 else lax.ppermute(hidden, "x", turn(size_x, k))
        rows = lax.dynamic_update_slice(rows, block[None], ((here - k) % size_x, 0, 0))
    rows = rows.reshape(token_count, both)
    partial, rows = lax.optimization_barrier((trade(partial, ("y", "zl")), rows))
    out_share = (jnp.sum(partial.astype(f32), axis=0) * scale_out).astype(bf16)
    out_share = out_share.reshape(rows_share, size_x, width)
    sends = jnp.stack(
        [lax.dynamic_index_in_dim(out_share, (here - place) % size_x, 1, False) for place in range(size_x)]
    )
    sends = jnp.broadcast_to(sends[:, None], (size_x, chips, rows_share, width))
    out = trade(sends.reshape(-1, rows_share, width), ("x", "y", "zl")).reshape(token_count, width)
    d_out = (error_gain * (out.astype(f32) - targets.astype(f32))).astype(bf16)

    def grad(hidden_part):
        return jnp.dot(hidden_part.T, d_out, preferred_element_type=f32) * scale_out

    grad_sent = grad(rows[:, unit_count:]).astype(bf16)
    grad_own = grad(rows[:, :unit_count])
    noise_own = lax.dynamic_index_in_dim(noise, core, 0, False).astype(f32)
    noise_other = lax.dynamic_index_in_dim(noise, 1 - core, 0, False).astype(f32) * (0.5 * inv_sigma)
    momentum_own = beta_one * momentum + (1.0 - beta_one) * 0.5 * grad_own
    curv_own = grad_own * noise_own * (0.5 * inv_sigma)
    spread_gain = 0.5 * (1.0 - beta_two) ** 2 / (hessian + weight_decay)
    grad_other, momentum_own, curv_own, noise_other, spread_gain = lax.optimization_barrier(
        (lax.ppermute(grad_sent, "c", SWAP), momentum_own, curv_own, noise_other, spread_gain)
    )
    grad_other = grad_other.astype(f32)
    new_momentum = momentum_own + (1.0 - beta_one) * 0.5 * grad_other
    curv_mean = curv_own + grad_other * noise_other
    spread = hessian - curv_mean
    new_hessian = beta_two * hessian + (1.0 - beta_two) * curv_mean + spread_gain * spread * spread
    new_means = means - step_rate * (new_momentum + weight_decay * means) / (
        new_hessian + weight_decay
    )
    return (new_means, new_hessian, new_momentum)


def solution(mesh):
    fine = Mesh(mesh.devices.reshape(SHAPE), ("y", "zl", "c", "zh", "x"))
    dp, fsdp = ("y", "zl", "c"), ("zh", "x")
    in_specs = (
        P(None, fsdp),
        P(None, fsdp),
        P(None, dp, fsdp),
        P(None, dp, fsdp),
        P(dp, fsdp),
        P(dp, fsdp),
        P(dp, fsdp),
        P(None, dp, fsdp),
    )
    out_specs = (P(dp, fsdp), P(dp, fsdp), P(dp, fsdp))
    return jax.shard_map(shards, mesh=fine, in_specs=in_specs, out_specs=out_specs, check_vma=False)
```

```python
import math

import jax
import jax.numpy as jnp
from jax import lax
from jax.experimental import pallas as pl
from jax.experimental.pallas import tpu as pltpu
from jax.sharding import Mesh, PartitionSpec as P

D = 8192


prior_size = 16.0
weight_decay = 0.001
beta_one = 0.9
beta_two = 0.95
step_rate = 0.2
loss_gain = 300.0

bf16 = jnp.bfloat16
f32 = jnp.float32
SHAPE = (8, 3, 2, 4, 4)
SWAP = [(0, 1), (1, 0)]


def trade(parts, axis):
    return lax.all_to_all(parts, axis, 0, 0, tiled=True)


def turn(size, steps):
    return [(i, (i + steps) % size) for i in range(size)]


def terms_kernel(tokens_ref, gate_ref, up_ref, terms_ref):
    rows = tokens_ref[...]
    both = gate_ref.shape[0]
    for place, weights_ref in ((0, gate_ref), (both, up_ref)):
        terms_ref[:, place : place + both] = lax.dot_general(
            rows, weights_ref[...], (((1,), (1,)), ((), ())), preferred_element_type=f32
        ).astype(bf16)


def gate_up_terms(tokens, gate_weights, up_weights, blocks):
    count, width = tokens.shape
    both = gate_weights.shape[0]
    return pl.pallas_call(
        terms_kernel,
        grid=(blocks,),
        in_specs=[
            pl.BlockSpec((count // blocks, width), lambda i: (i, 0)),
            pl.BlockSpec((both, width), lambda i: (0, 0)),
            pl.BlockSpec((both, width), lambda i: (0, 0)),
        ],
        out_specs=pl.BlockSpec((count // blocks, 2 * both), lambda i: (i, 0)),
        out_shape=jax.ShapeDtypeStruct((count, 2 * both), bf16),
        compiler_params=pltpu.CompilerParams(vmem_limit_bytes=56 * 1024 * 1024),
    )(tokens, gate_weights, up_weights)


def shards(tokens, targets, gate_weights, up_weights, means, hessian, momentum, noise):
    token_count = tokens.shape[0]
    width = tokens.shape[1]
    unit_count = means.shape[0]
    size_x, size_zh = lax.axis_size("x"), lax.axis_size("zh")
    size_y, size_zl, size_c = lax.axis_size("y"), lax.axis_size("zl"), lax.axis_size("c")
    hidden_count = unit_count * size_y * size_zl * size_c
    scale_in = 1.0 / math.sqrt(D)
    scale_out = 1.0 / math.sqrt(hidden_count)
    error_gain = loss_gain / math.sqrt(token_count)
    both = 2 * unit_count
    core = lax.axis_index("c")

    terms = gate_up_terms(
        tokens, gate_weights.reshape(both, width), up_weights.reshape(both, width), 2
    )
    terms = trade(terms.reshape(size_x, -1, 2 * both), "x")
    terms = jnp.sum(terms.astype(f32), axis=0).astype(bf16)

    inv_sigma = jnp.sqrt(prior_size * (hessian + weight_decay))
    samples = (means[None] + noise.astype(f32) / inv_sigma[None]).astype(bf16)
    weights_own = lax.dynamic_index_in_dim(samples, core, 0, False)
    weights_other = lax.ppermute(lax.dynamic_index_in_dim(samples, 1 - core, 0, False), "c", SWAP)
    weights = jnp.concatenate([weights_own, weights_other], axis=0)
    terms, weights = lax.optimization_barrier((terms, weights))
    wide = jnp.concatenate([weights] + [lax.ppermute(weights, "x", turn(size_x, k)) for k in range(1, size_x)], axis=1)

    terms = trade(terms.reshape(size_zh, -1, 2 * both), "zh")
    sums = jnp.sum(terms.astype(f32), axis=0) * scale_in
    gate_sum, up_sum = sums[:, :both], sums[:, both:]
    hidden_share = (gate_sum * jax.nn.sigmoid(gate_sum) * up_sum).astype(bf16)
    share = hidden_share.shape[0]
    parts = jnp.stack([hidden_share[:, :unit_count], hidden_share[:, unit_count:]])
    parts = jnp.broadcast_to(parts[:, None], (size_c, size_zh, share, unit_count))
    hidden = trade(parts.reshape(-1, share, unit_count), ("c", "zh"))
    rows_x = size_zh * share
    hidden = hidden.reshape(size_c, rows_x, unit_count)
    hidden_own = lax.dynamic_index_in_dim(hidden, core, 0, False)
    hidden_other = lax.dynamic_index_in_dim(hidden, 1 - core, 0, False)

    partial = jnp.dot(hidden_own, wide[:unit_count], preferred_element_type=f32) + jnp.dot(
        hidden_other, wide[unit_count:], preferred_element_type=f32
    )
    chips = size_y * size_zl
    rows_share = rows_x // chips
    partial = partial.astype(bf16).reshape(chips, rows_share, size_x * width)
    hidden, partial = lax.optimization_barrier((hidden, partial))
    here = lax.axis_index("x")
    rows = jnp.zeros((size_c, size_x, rows_x, unit_count), bf16)
    for k in range(size_x):
        block = hidden if k == 0 else lax.ppermute(hidden, "x", turn(size_x, k))
        rows = lax.dynamic_update_slice(rows, block[:, None], (0, (here - k) % size_x, 0, 0))
    rows = rows.reshape(size_c, token_count, unit_count)
    rows_own = lax.dynamic_index_in_dim(rows, core, 0, False)
    rows_other = lax.dynamic_index_in_dim(rows, 1 - core, 0, False)

    partial, rows_own, rows_other = lax.optimization_barrier(
        (trade(partial, ("y", "zl")), rows_own, rows_other)
    )
    out_share = (jnp.sum(partial.astype(f32), axis=0) * scale_out).astype(bf16)
    out_share = out_share.reshape(rows_share, size_x, width)
    sends = jnp.stack(
        [lax.dynamic_index_in_dim(out_share, (here - place) % size_x, 1, False) for place in range(size_x)]
    )
    sends = jnp.broadcast_to(sends[:, None], (size_x, chips, rows_share, width))
    out = trade(sends.reshape(-1, rows_share, width), ("x", "y", "zl")).reshape(token_count, width)
    d_out = (error_gain * (out.astype(f32) - targets.astype(f32))).astype(bf16)

    def grad(hidden_part):
        return jnp.dot(hidden_part.T, d_out, preferred_element_type=f32) * scale_out

    grad_sent = grad(rows_other)
    grad_own = grad(rows_own)
    noise_own = lax.dynamic_index_in_dim(noise, core, 0, False).astype(f32)
    noise_other = lax.dynamic_index_in_dim(noise, 1 - core, 0, False).astype(f32) * (0.5 * inv_sigma)
    momentum_own = beta_one * momentum + (1.0 - beta_one) * 0.5 * grad_own
    curv_own = grad_own * noise_own * (0.5 * inv_sigma)
    spread_gain = 0.5 * (1.0 - beta_two) ** 2 / (hessian + weight_decay)
    grad_other, momentum_own, curv_own, noise_other, spread_gain = lax.optimization_barrier(
        (lax.ppermute(grad_sent.astype(bf16), "c", SWAP), momentum_own, curv_own, noise_other, spread_gain)
    )
    grad_other = grad_other.astype(f32)
    new_momentum = momentum_own + (1.0 - beta_one) * 0.5 * grad_other
    curv_mean = curv_own + grad_other * noise_other
    spread = hessian - curv_mean
    new_hessian = beta_two * hessian + (1.0 - beta_two) * curv_mean + spread_gain * spread * spread
    new_means = means - step_rate * (new_momentum + weight_decay * means) / (
        new_hessian + weight_decay
    )
    return (new_means, new_hessian, new_momentum)


def solution(mesh):
    fine = Mesh(mesh.devices.reshape(SHAPE), ("y", "zl", "c", "zh", "x"))
    dp, fsdp = ("y", "zl", "c"), ("zh", "x")
    in_specs = (
        P(None, fsdp),
        P(None, fsdp),
        P(None, dp, fsdp),
        P(None, dp, fsdp),
        P(dp, fsdp),
        P(dp, fsdp),
        P(dp, fsdp),
        P(None, dp, fsdp),
    )
    out_specs = (P(dp, fsdp), P(dp, fsdp), P(dp, fsdp))
    return jax.shard_map(shards, mesh=fine, in_specs=in_specs, out_specs=out_specs, check_vma=False)
```
